512 devices in a mesh: dp: 32 (over x, z_lo, core), tm: 16 (over y, z_hi).
Axes of the slice: x: 4, y: 8, z: 8 (z_hi: 2, z_lo: 4; z = z_hi * 4 + z_lo), core: 2. Of those that a mesh axis runs over, the one named last changes fastest.
Arguments:
- video: bfloat16 [32, 64, 64, 640], P('dp', 'tm'), may hold values from -6 to 6
- cotangent: bfloat16 [32, 64, 64, 640], P('dp', 'tm'), may hold values from -6 to 6
- spatial_weight: bfloat16 [9, 640, 640], P(None, 'tm'), may hold values from -0.078125 to 0.078125
- temporal_weight: bfloat16 [3, 640, 640], replicated, may hold values from -0.125 to 0.125
- proj_weight: bfloat16 [640, 640], replicated, may hold values from -0.25 to 0.25
Outputs:
- block_out: bfloat16 [32, 64, 64, 640], P('dp', 'tm')
- video_grad: bfloat16 [32, 64, 64, 640], P('dp', 'tm')
- proj_grad: float32 [640, 640], P('tm')
The draws below stay inside these ranges and needn't reach their ends.
All inputs are finite; a program needn't handle non-finite values.
Results may differ from the reference program's by a relative error of at most 0.03.
Values may be sent and summed in bfloat16 or wider, within the bound.
No kernel may reach another device: no remote copies, remote signals or barrier semaphores. Data moves between devices by JAX's collectives and lax.ppermute only.
A program may use at most 64 MiB of HBM per device.

```python
import math
import jax
import jax.numpy as jnp
from jax import lax

C = 640
HGT = 8
WID = 8
CLIPS = 32
FRAMES = 64


def spiked(drawn, key, source, target, parts, factor):
    owner, partner = [(jnp.arange(drawn.shape[position]) // (drawn.shape[position] // parts)).reshape([-1 if axis == position else 1 for axis in range(drawn.ndim)]) for position in (source, target)]
    chosen = jax.random.permutation(key, parts)[partner]
    strong = (owner == chosen) | (owner == (partner + parts // 2) % parts)
    return jnp.where(strong, factor * drawn, drawn)


def block_scale(stream_key, dims, shards, least, largest):
    level, own = 1.0, jax.random.fold_in(stream_key, 6)
    for dim, parts in shards:
        steps = jnp.exp(jax.random.uniform(jax.random.fold_in(own, dim), (parts,), jnp.float32, least / len(shards), largest / len(shards)))
        level = level * jnp.repeat(steps, dims[dim] // parts).reshape([-1 if axis == dim else 1 for axis in range(len(dims))])
    return level


def gaussian(own_key, dims, scale, reach, cuts=(), held_as=jnp.bfloat16):
    drawn = jax.random.normal(own_key, dims, jnp.float32) * scale
    if len(cuts) > 0:
        drawn = block_scale(own_key, dims, cuts, -0.22, 0.18) * drawn
    return jnp.clip(drawn, min=-reach, max=reach).astype(held_as)


def gaussian_with(stream_key, dims, scale, most, shards, heavy, dtype=jnp.bfloat16):
    drawn = scale * jax.random.normal(stream_key, dims, jnp.float32)
    if shards:
        drawn = drawn * block_scale(stream_key, dims, shards, -0.22, 0.18)
    return jnp.clip(spiked(drawn, jax.random.fold_in(stream_key, 3), *heavy), -most, most).astype(dtype)


def setup_inputs(seed: int = 0) -> dict:
    key_of = jax.random.split(jax.random.key(seed), 6)
    video = gaussian(key_of[0], (CLIPS, FRAMES, HGT * WID, C), 1.0, 6.0, ((0, 32), (1, 16)))
    cotangent = gaussian_with(key_of[1], (CLIPS, FRAMES, HGT * WID, C), 1.0, 6.0, ((0, 32), (1, 16)), (0, 3, 32, 2.75))
    spatial_weight = gaussian(key_of[2], (9, C, C), (9 * C) ** -0.5, 0.078125, ((1, 16),))
    temporal_weight = gaussian(key_of[3], (3, C, C), (3 * C) ** -0.5, 0.125)
    proj_weight = gaussian(key_of[4], (C, C), C ** -0.5, 0.25)
    return dict(video=video, cotangent=cotangent, spatial_weight=spatial_weight, temporal_weight=temporal_weight, proj_weight=proj_weight)


def silu_grad(values):
    sigmoid = jax.nn.sigmoid(values)
    return sigmoid * (1.0 + values * (1.0 - sigmoid))

def patches(volume, orient):
    grid_rows, grid_cols = (volume.shape[1], volume.shape[2])
    padded = jnp.pad(volume, ((0, 0), (1, 1), (1, 1), (0, 0)))
    pieces = []
    for row_off in (-1, 0, 1):
        for col_off in (-1, 0, 1):
            row_start = 1 + orient * row_off
            col_start = 1 + orient * col_off
            pieces.append(padded[:, row_start:row_start + grid_rows, col_start:col_start + grid_cols, :])
    return jnp.stack(pieces, axis=3)

def reference(video, cotangent, spatial_weight, temporal_weight, proj_weight):
    channels = video.shape[-1]
    frame_count = video.shape[1]
    kernel_rows = spatial_weight.reshape(9 * channels, channels)
    kernel_back = jnp.transpose(spatial_weight, (0, 2, 1)).reshape(9 * channels, channels)

    def one_clip(clip_pair):
        clip_in, grad_clip = clip_pair
        in_rows = clip_in.reshape(-1, channels).astype(jnp.float32)
        volume = clip_in.reshape(frame_count, HGT, WID, channels)
        act = jax.nn.silu(volume.astype(jnp.float32)).astype(jnp.bfloat16)
        spatial = jnp.dot(patches(act, 1).reshape(-1, 9 * channels), kernel_rows, preferred_element_type=jnp.float32)
        spatial = spatial.astype(jnp.bfloat16).reshape(frame_count, HGT * WID, channels)
        padded = jnp.pad(spatial, ((2, 2), (0, 0), (0, 0)))
        temporal = jnp.zeros((frame_count * HGT * WID, channels), jnp.float32)
        for tap_index in range(3):
            shifted = padded[2 * tap_index:2 * tap_index + frame_count].reshape(-1, channels)
            temporal = temporal + jnp.dot(shifted, temporal_weight[tap_index], preferred_element_type=jnp.float32)
        temporal = temporal.astype(jnp.bfloat16).astype(jnp.float32)
        gated = jax.nn.silu(temporal).astype(jnp.bfloat16)
        block = (in_rows + jnp.dot(gated, proj_weight, preferred_element_type=jnp.float32)).astype(jnp.bfloat16)
        grad_rows = grad_clip.reshape(-1, channels)
        gated_grad = jnp.dot(grad_rows, proj_weight.T, preferred_element_type=jnp.float32) * silu_grad(temporal)
        gated_grad = gated_grad.astype(jnp.bfloat16).reshape(frame_count, HGT * WID, channels)
        grad_pad = jnp.pad(gated_grad, ((2, 2), (0, 0), (0, 0)))
        spatial_grad = jnp.zeros((frame_count * HGT * WID, channels), jnp.float32)
        for tap_index in range(3):
            shifted = grad_pad[4 - 2 * tap_index:4 - 2 * tap_index + frame_count].reshape(-1, channels)
            spatial_grad = spatial_grad + jnp.dot(shifted, temporal_weight[tap_index].T, preferred_element_type=jnp.float32)
        spatial_grad = spatial_grad.astype(jnp.bfloat16).reshape(frame_count, HGT, WID, channels)
        act_grad = jnp.dot(patches(spatial_grad, -1).reshape(-1, 9 * channels), kernel_back, preferred_element_type=jnp.float32)
        video_grad = (grad_rows.astype(jnp.float32) + act_grad * silu_grad(in_rows)).astype(jnp.bfloat16)
        partial_value = jnp.dot(gated.T, grad_rows, preferred_element_type=jnp.float32)
        return (block.reshape(clip_in.shape), video_grad.reshape(clip_in.shape), partial_value)
    block_out, video_grad, partials = lax.map(one_clip, (video, cotangent))
    factor = 1.0 / math.sqrt(CLIPS * FRAMES * HGT * WID)
    proj_grad = lax.optimization_barrier(jnp.sum(partials, axis=0)) * factor
    return (block_out, video_grad, proj_grad)
```

```python
import functools
import math

import jax
import jax.numpy as jnp
from jax import lax
from jax.experimental import pallas as pl
from jax.experimental.pallas import tpu as pltpu
from jax.sharding import Mesh
from jax.sharding import PartitionSpec as P

C = 640
ROWS = 256
HALO = 128
EXT = ROWS + 2 * HALO
PIECE = 768
HALF = PIECE // 2
LEFT = 384
TAIL = PIECE - C
PIECES = 8
TM = 16
SHARD = 40
VMEM = 50 * 1024 * 1024
F32 = jnp.float32
BF16 = jnp.bfloat16
TAPS = [(di, dj) for di in (-1, 0, 1) for dj in (-1, 0, 1)]


def sigmoid(values):
    return 1.0 / (1.0 + jnp.exp(-values))


def silu_grad(values):
    s = sigmoid(values)
    return s * (1.0 + values * (1.0 - s))


def shifted(values, di, dj):
    rows = values.shape[0]
    step = 8 * di + dj
    moved = values if step == 0 else pltpu.roll(values, (-step) % rows, 0)
    if step == 0:
        return moved
    row = lax.broadcasted_iota(jnp.int32, values.shape, 0)
    i = (row // 8) % 8 + di
    j = row % 8 + dj
    inside = (i >= 0) & (i < 8) & (j >= 0) & (j < 8)
    return jnp.where(inside, moved, 0.0)


def prep_kernel(video_ref, spread_ref, out_ref):
    x = video_ref[...].astype(F32)
    act = (x * sigmoid(x)).astype(BF16).astype(F32)
    last = shifted(act, *TAPS[8]).astype(BF16)
    tail = jnp.dot(last, spread_ref[...], preferred_element_type=F32).astype(BF16)
    for tap in range(PIECES):
        out_ref[tap, :, :C] = shifted(act, *TAPS[tap]).astype(BF16)
        out_ref[tap, :, C:] = tail[:, tap * TAIL : (tap + 1) * TAIL]


def prep(video_ext, spread):
    chunk = 128
    return pl.pallas_call(
        prep_kernel,
        grid=(EXT // chunk,),
        in_specs=[
            pl.BlockSpec((chunk, C), lambda n: (n, 0)),
            pl.BlockSpec((C, PIECES * TAIL), lambda n: (0, 0)),
        ],
        out_specs=pl.BlockSpec((PIECES, chunk, PIECE), lambda n: (0, n, 0)),
        out_shape=jax.ShapeDtypeStruct((PIECES, EXT, PIECE), BF16),
        compiler_params=pltpu.CompilerParams(vmem_limit_bytes=VMEM),
        cost_estimate=pl.CostEstimate(flops=2 * EXT * C * PIECES * TAIL, bytes_accessed=20 * 1024 * 1024, transcendentals=0),
        name="patches",
    )(video_ext, spread)


def weight_copies(place_ref, refs, which, held, sems, index):
    quarter, start = place_ref[0], place_ref[2]
    first, second = refs
    copies = []
    for n in range(4):
        left = (start + n) % 4
        right = (quarter + n) % 4
        pair = (
            pltpu.make_async_copy(
                first.at[n], held.at[index(left, which), :, pl.ds(0, LEFT)], sems.at[2 * n]
            ),
            pltpu.make_async_copy(
                second.at[n], held.at[index(right, which), :, pl.ds(LEFT, C - LEFT)], sems.at[2 * n + 1]
            ),
        )
        for copy in pair:
            copy.start()
        copies += pair
    return copies


def spatial_sum(patch_ref, which, patches, patch_sems, held, copies):
    patch_copies = []
    for quarter in range(4):
        copy = pltpu.make_async_copy(
            patch_ref.at[2 * quarter + which], patches.at[quarter], patch_sems.at[quarter]
        )
        copy.start()
        patch_copies.append(copy)
    for copy in copies + patch_copies:
        copy.wait()
    value = jnp.dot(patches[0], held[0], preferred_element_type=F32)
    for quarter in range(1, 4):
        value += jnp.dot(patches[quarter], held[quarter], preferred_element_type=F32)
    return value


def one_core(quarter, which):
    return quarter


def both_cores(quarter, which):
    return 2 * quarter + which


def partial_kernel(place_ref, first, second, patch_ref, out_ref, held, patches, sems, patch_sems):
    core = place_ref[1]
    copies = weight_copies(place_ref, (first, second), core, held, sems, one_core)
    out_ref[...] = spatial_sum(patch_ref, core, patches, patch_sems, held, copies)


def forward_kernel(place_ref, first, second, patch_ref, *refs):
    partial_ref, video_ref, cot_ref, temporal_ref, proj_ref, order_ref = refs[:6]
    block_ref, gg_ref, keep_ref, give_ref = refs[6:10]
    held, patches, sems, patch_sems = refs[10:]
    core = 1 - place_ref[1]
    copies = weight_copies(place_ref, (first, second), core, held, sems, one_core)
    total = spatial_sum(patch_ref, core, patches, patch_sems, held, copies) + partial_ref[...]
    spatial = total.astype(BF16)
    temporal = jnp.dot(spatial[:ROWS], temporal_ref[0], preferred_element_type=F32)
    for m in (1, 2):
        temporal += jnp.dot(
            spatial[m * HALO : m * HALO + ROWS], temporal_ref[m], preferred_element_type=F32
        )
    temporal = temporal.astype(BF16).astype(F32)
    s = sigmoid(temporal)
    gated = (temporal * s).astype(BF16)
    cot = cot_ref[...]
    ordered = jnp.dot(gated, order_ref[...], preferred_element_type=F32).astype(BF16)
    part = lax.dot_general(
        ordered, cot, (((0,), (0,)), ((), ())), preferred_element_type=F32
    ).astype(BF16)
    keep_ref[...] = part[:HALF]
    give_ref[...] = part[HALF:]
    back = lax.dot_general(
        cot, proj_ref[...], (((1,), (1,)), ((), ())), preferred_element_type=F32
    )
    gg_ref[...] = (back * (s * (1.0 + temporal * (1.0 - s)))).astype(BF16)
    branch = jnp.dot(gated, proj_ref[...], preferred_element_type=F32)
    block_ref[...] = (video_ref[...].astype(F32) + branch).astype(BF16)


def backward_kernel(place_ref, first, second, other_first, other_second, *refs):
    ext_ref, video_ref, cot_ref, temporal_ref, spread_ref = refs[:5]
    out_ref = refs[5]
    held, tail, total, sems, other_sems = refs[6:]
    core = place_ref[1]
    copies = weight_copies(place_ref, (first, second), core, held, sems, both_cores)
    copies += weight_copies(
        place_ref, (other_first, other_second), 1 - core, held, other_sems, both_cores
    )
    ext = ext_ref[...]
    nt = (((1,), (1,)), ((), ()))
    grad = lax.dot_general(ext[2 * HALO :], temporal_ref[0], nt, preferred_element_type=F32)
    grad += lax.dot_general(
        ext[HALO : HALO + ROWS], temporal_ref[1], nt, preferred_element_type=F32
    )
    grad += lax.dot_general(ext[:ROWS], temporal_ref[2], nt, preferred_element_type=F32)
    grad = grad.astype(BF16).astype(F32)
    for copy in copies:
        copy.wait()
    last = shifted(grad, -TAPS[8][0], -TAPS[8][1]).astype(BF16)
    for tap in range(PIECES):
        moved = shifted(grad, -TAPS[tap][0], -TAPS[tap][1]).astype(BF16)
        value = lax.dot_general(moved, held[tap, :C], nt, preferred_element_type=F32)
        if tap == 0:
            total[...] = value
        else:
            total[...] += value
        tail[:, tap * TAIL : (tap + 1) * TAIL] = lax.dot_general(
            last, held[tap, C:], nt, preferred_element_type=F32
        ).astype(BF16)
    total[...] += lax.dot_general(tail[...], spread_ref[...], nt, preferred_element_type=F32)
    video = video_ref[...].astype(F32)
    out_ref[...] = (
        cot_ref[...].astype(F32) + total[...] * silu_grad(video)
    ).astype(BF16)


def whole():
    return pl.BlockSpec(memory_space=pltpu.VMEM)


def anywhere():
    return pl.BlockSpec(memory_space=pl.ANY)


def partial(place, weights, patches):
    return pl.pallas_call(
        partial_kernel,
        in_specs=[pl.BlockSpec(memory_space=pltpu.SMEM)] + [anywhere()] * 3,
        out_specs=whole(),
        out_shape=jax.ShapeDtypeStruct((EXT, C), F32),
        scratch_shapes=[
            pltpu.VMEM((4, PIECE, C), BF16),
            pltpu.VMEM((4, EXT, PIECE), BF16),
            pltpu.SemaphoreType.DMA((8,)),
            pltpu.SemaphoreType.DMA((4,)),
        ],
        compiler_params=pltpu.CompilerParams(vmem_limit_bytes=VMEM),
        cost_estimate=pl.CostEstimate(
            flops=EXT * PIECES * PIECE * C, bytes_accessed=8 * 1024 * 1024, transcendentals=0
        ),
        name="partial",
    )(place, *weights, patches)


def forward(place, weights, patches, summed, video, cot, temporal_weight, proj_weight, order):
    return pl.pallas_call(
        forward_kernel,
        in_specs=[pl.BlockSpec(memory_space=pltpu.SMEM)] + [anywhere()] * 3 + [whole()] * 6,
        out_specs=[whole()] * 4,
        out_shape=[
            jax.ShapeDtypeStruct((ROWS, C), BF16),
            jax.ShapeDtypeStruct((ROWS, C), BF16),
            jax.ShapeDtypeStruct((HALF, C), BF16),
            jax.ShapeDtypeStruct((HALF, C), BF16),
        ],
        scratch_shapes=[
            pltpu.VMEM((4, PIECE, C), BF16),
            pltpu.VMEM((4, EXT, PIECE), BF16),
            pltpu.SemaphoreType.DMA((8,)),
            pltpu.SemaphoreType.DMA((4,)),
        ],
        compiler_params=pltpu.CompilerParams(vmem_limit_bytes=VMEM),
        cost_estimate=pl.CostEstimate(
            flops=2 * EXT * PIECES * PIECE * C, bytes_accessed=20 * 1024 * 1024, transcendentals=0
        ),
        name="forward",
    )(place, *weights, patches, summed, video, cot, temporal_weight, proj_weight, order)


def backward(place, weights, ext, video, cot, temporal_weight, spread):
    return pl.pallas_call(
        backward_kernel,
        in_specs=[pl.BlockSpec(memory_space=pltpu.SMEM)] + [anywhere()] * 4 + [whole()] * 5,
        out_specs=whole(),
        out_shape=jax.ShapeDtypeStruct((ROWS, C), BF16),
        scratch_shapes=[
            pltpu.VMEM((PIECES, PIECE, C), BF16),
            pltpu.VMEM((ROWS, PIECES * TAIL), BF16),
            pltpu.VMEM((ROWS, C), F32),
            pltpu.SemaphoreType.DMA((8,)),
            pltpu.SemaphoreType.DMA((8,)),
        ],
        compiler_params=pltpu.CompilerParams(vmem_limit_bytes=VMEM),
        cost_estimate=pl.CostEstimate(
            flops=2 * ROWS * PIECES * PIECE * C, bytes_accessed=30 * 1024 * 1024, transcendentals=0
        ),
        name="backward",
    )(place, *weights, ext, video, cot, temporal_weight, spread)


def next_quarter(values, r):
    def step(c):
        return (0, 1, 2 if c == 0 else -2, -1)[r]

    pairs = [(c * 8 + (y + step(c)) % 8, c * 8 + y) for y in range(8) for c in range(2)]
    return lax.ppermute(values, ("c", "y"), pairs)


def paired(values):
    groups = [
        [(zl if zh == 0 else 3 - zl) * 16 + y * 2 + zh for y in range(8) for zh in range(2)]
        for zl in range(4)
    ]
    return lax.all_to_all(
        values, ("zl", "y", "zh"), split_axis=0, concat_axis=0, axis_index_groups=groups, tiled=True
    )


def other_core(values):
    return lax.ppermute(values, "c", [(0, 1), (1, 0)])


def halos(rows):
    tm = ("y", "zh")
    before = lax.ppermute(rows[ROWS - HALO :], tm, [(t, t + 1) for t in range(TM - 1)])
    after = lax.ppermute(rows[:HALO], tm, [(t + 1, t) for t in range(TM - 1)])
    return before, after


def spread_matrix():
    k = lax.broadcasted_iota(jnp.int32, (C, PIECES * TAIL), 0)
    lane = lax.broadcasted_iota(jnp.int32, (C, PIECES * TAIL), 1)
    j, t, i = lane // TAIL, (lane % TAIL) // 8, lane % 8
    return ((i < 5) & (k == SHARD * t + 5 * j + i)).astype(BF16)


def order_matrix(core):
    k = lax.broadcasted_iota(jnp.int32, (C, PIECE), 0)
    lane = lax.broadcasted_iota(jnp.int32, (C, PIECE), 1)
    h, t, i = (lane // HALF + core) % 2, (lane % HALF) // 24, lane % 24
    return ((i < 20) & (k == SHARD * t + 20 * h + i)).astype(BF16)


def local(video, cotangent, spatial_weight, temporal_weight, proj_weight):
    core = lax.axis_index("c")
    x, y, zl, zh = (lax.axis_index(name) for name in ("x", "y", "zl", "zh"))
    quarter = (x + y + zl) % 4
    place = jnp.stack([quarter, core, (y + zl) % 4]).astype(jnp.int32)

    rows = video.reshape(ROWS, C)
    cot = cotangent.reshape(ROWS, C)

    main = spatial_weight[:8].reshape(4, 2, SHARD, C)
    tail = spatial_weight[8].reshape(4, 2, 5, C)
    main = lax.dynamic_index_in_dim(main, core, 1, keepdims=False)
    tail = lax.dynamic_index_in_dim(tail, core, 1, keepdims=False)
    quarters = jnp.concatenate([main, tail, jnp.zeros((4, 3, C), BF16)], axis=1)
    quarters = jnp.concatenate([quarters, quarters], axis=0)
    low = lax.dynamic_slice_in_dim(quarters, (x + jnp.where(zh == 0, zl, 3 - zl)) % 4, 4, 0)
    high = lax.dynamic_slice_in_dim(quarters, (x + jnp.where(zh == 0, 3 - zl, zl)) % 4, 4, 0)
    sent = jnp.stack([low, high], axis=1)
    sent = jnp.broadcast_to(sent[None], (2, 4, 2, 48, C)).reshape(TM, 48, C)

    def rowed(got):
        width = got.shape[2]
        return jnp.concatenate(
            [got[:, :SHARD].reshape(C, width), got[:, SHARD:].reshape(TAIL, width)], axis=0
        )

    got, shared = lax.optimization_barrier((paired(sent), rows))
    left, right = rowed(got[:, :, :LEFT]), rowed(got[:, :, LEFT:])
    first = lax.all_to_all(
        jnp.broadcast_to(left[None], (4, PIECE, LEFT)), "x", split_axis=0, concat_axis=0, tiled=True
    )
    second = [right] + [next_quarter(right, r) for r in (1, 2, 3)]
    before, after = halos(shared)
    spread = spread_matrix()
    patches = prep(jnp.concatenate([before, rows, after], axis=0), spread)
    first, patches, *second = lax.optimization_barrier((first, patches, *second))
    weights = [first, jnp.stack(second)]
    others = [other_core(v) for v in weights]

    summed = partial(place, weights, patches)
    block_out, gated_grad, keep, give = forward(
        place, others, patches, summed, rows, cot, temporal_weight, proj_weight, order_matrix(core)
    )

    before, after = halos(gated_grad)
    pair = (keep.astype(F32) + other_core(give).astype(F32)).astype(BF16)
    blocks = paired(pair.reshape(TM, 24, C))
    blocks, before, after = lax.optimization_barrier((blocks, before, after))
    ext = jnp.concatenate([before, gated_grad, after], axis=0)
    video_grad = backward(place, weights + others, ext, rows, cot, temporal_weight, spread)

    block = jnp.sum(blocks.astype(F32), axis=0).astype(BF16)
    sent = jnp.broadcast_to(block[None], (16, 24, C))
    copies = lax.all_to_all(sent, ("x", "zl"), split_axis=0, concat_axis=0, tiled=True)
    copies, video_grad = lax.optimization_barrier((copies, video_grad))
    summed = jnp.sum(copies.astype(F32), axis=0)
    theirs = other_core(summed)
    low = jnp.where(core == 0, summed, theirs)[:20]
    high = jnp.where(core == 0, theirs, summed)[:20]
    factor = 1.0 / math.sqrt(ROWS * 512)
    proj_grad = jnp.concatenate([low, high], axis=0) * factor
    return (block_out.reshape(video.shape), video_grad.reshape(video.shape), proj_grad)


def solution(mesh):
    fine = Mesh(mesh.devices.reshape(4, 4, 2, 8, 2), ("x", "zl", "c", "y", "zh"))
    dp, tm = ("x", "zl", "c"), ("y", "zh")
    in_specs = (P(dp, tm, None, None), P(dp, tm, None, None), P(None, tm, None), P(), P())
    out_specs = (P(dp, tm, None, None), P(dp, tm, None, None), P(tm, None))
    return jax.shard_map(local, mesh=fine, in_specs=in_specs, out_specs=out_specs, check_vma=False)
```

```python
import functools
import math

import jax
import jax.numpy as jnp
from jax import lax
from jax.experimental import pallas as pl
from jax.experimental.pallas import tpu as pltpu
from jax.sharding import Mesh
from jax.sharding import PartitionSpec as P

C = 640
ROWS = 256
HALO = 128
EXT = ROWS + 2 * HALO
PIECE = 768
HALF = PIECE // 2
LEFT = 512
TAIL = PIECE - C
PIECES = 8
TM = 16
SHARD = 40
VMEM = 50 * 1024 * 1024
F32 = jnp.float32
BF16 = jnp.bfloat16
TAPS = [(di, dj) for di in (-1, 0, 1) for dj in (-1, 0, 1)]


def sigmoid(values):
    return 1.0 / (1.0 + jnp.exp(-values))


def silu_grad(values):
    s = sigmoid(values)
    return s * (1.0 + values * (1.0 - s))


def shifted(values, di, dj):
    rows = values.shape[0]
    step = 8 * di + dj
    moved = values if step == 0 else pltpu.roll(values, (-step) % rows, 0)
    if step == 0:
        return moved
    row = lax.broadcasted_iota(jnp.int32, values.shape, 0)
    i = (row // 8) % 8 + di
    j = row % 8 + dj
    inside = (i >= 0) & (i < 8) & (j >= 0) & (j < 8)
    return jnp.where(inside, moved, 0.0)


def prep_kernel(video_ref, spread_ref, out_ref):
    x = video_ref[...].astype(F32)
    act = (x * sigmoid(x)).astype(BF16).astype(F32)
    last = shifted(act, *TAPS[8]).astype(BF16)
    tail = jnp.dot(last, spread_ref[...], preferred_element_type=F32).astype(BF16)
    for tap in range(PIECES):
        out_ref[tap, :, :C] = shifted(act, *TAPS[tap]).astype(BF16)
        out_ref[tap, :, C:] = tail[:, tap * TAIL : (tap + 1) * TAIL]


def prep(video_ext, spread):
    chunk = 128
    return pl.pallas_call(
        prep_kernel,
        grid=(EXT // chunk,),
        in_specs=[
            pl.BlockSpec((chunk, C), lambda n: (n, 0)),
            pl.BlockSpec((C, PIECES * TAIL), lambda n: (0, 0)),
        ],
        out_specs=pl.BlockSpec((PIECES, chunk, PIECE), lambda n: (0, n, 0)),
        out_shape=jax.ShapeDtypeStruct((PIECES, EXT, PIECE), BF16),
        compiler_params=pltpu.CompilerParams(vmem_limit_bytes=VMEM),
        cost_estimate=pl.CostEstimate(flops=16 * EXT * C * PIECES * TAIL, bytes_accessed=20 * 1024 * 1024, transcendentals=0),
        name="patches",
    )(video_ext, spread)


def weight_copies(
    place_ref, refs, which, held, sems, index, patch_ref=None, patches=None, patch_sems=None
):
    own, start = place_ref[0], place_ref[2]
    first, second = refs
    copies = []
    for quarter in range(4):
        from_x = (quarter - start + 4) % 4
        from_y = (quarter - own + 4) % 4
        slot = index(quarter, which)
        pair = [
            pltpu.make_async_copy(
                first.at[from_x], held.at[slot, :, pl.ds(0, LEFT)], sems.at[2 * quarter]
            ),
            pltpu.make_async_copy(
                second.at[from_y], held.at[slot, :, pl.ds(LEFT, C - LEFT)], sems.at[2 * quarter + 1]
            ),
        ]
        if patch_ref is not None:
            pair.append(
                pltpu.make_async_copy(
                    patch_ref.at[2 * quarter + which], patches.at[quarter], patch_sems.at[quarter]
                )
            )
        for copy in pair:
            copy.start()
        copies.append(pair)
    return copies


def spatial_sum(patches, held, copies, total):
    for quarter in range(4):
        for copy in copies[quarter]:
            copy.wait()
        value = jnp.dot(patches[quarter], held[quarter], preferred_element_type=F32)
        if quarter == 0:
            total[...] = value
        else:
            total[...] += value


def one_core(quarter, which):
    return quarter


def both_cores(quarter, which):
    return 2 * quarter + which


def partial_kernel(place_ref, first, second, patch_ref, out_ref, held, patches, sems, patch_sems):
    core = place_ref[1]
    copies = weight_copies(
        place_ref, (first, second), core, held, sems, one_core, patch_ref, patches, patch_sems
    )
    spatial_sum(patches, held, copies, out_ref)


def forward_kernel(place_ref, first, second, patch_ref, *refs):
    given = refs[:6]
    block_ref, gg_ref, keep_ref, give_ref = refs[6:10]
    held, patches, total, sems, patch_sems, given_sems = refs[10:16]
    local = refs[16:]
    partial_ref, video_ref, cot_ref, temporal_ref, proj_ref, order_ref = local
    core = 1 - place_ref[1]
    copies = weight_copies(
        place_ref, (first, second), core, held, sems, one_core, patch_ref, patches, patch_sems
    )
    later = [
        pltpu.make_async_copy(given[n], local[n], given_sems.at[n]) for n in range(len(given))
    ]
    for copy in later:
        copy.start()
    spatial_sum(patches, held, copies, total)
    for copy in later:
        copy.wait()
    total = total[...] + partial_ref[...]
    spatial = total.astype(BF16)
    temporal = jnp.dot(spatial[:ROWS], temporal_ref[0], preferred_element_type=F32)
    for m in (1, 2):
        temporal += jnp.dot(
            spatial[m * HALO : m * HALO + ROWS], temporal_ref[m], preferred_element_type=F32
        )
    temporal = temporal.astype(BF16).astype(F32)
    s = sigmoid(temporal)
    gated = (temporal * s).astype(BF16)
    cot = cot_ref[...]
    ordered = jnp.dot(gated, order_ref[...], preferred_element_type=F32).astype(BF16)
    part = lax.dot_general(
        ordered, cot, (((0,), (0,)), ((), ())), preferred_element_type=F32
    ).astype(BF16)
    keep_ref[...] = part[:HALF]
    give_ref[...] = part[HALF:]
    back = lax.dot_general(
        cot, proj_ref[...], (((1,), (1,)), ((), ())), preferred_element_type=F32
    )
    gg_ref[...] = (back * (s * (1.0 + temporal * (1.0 - s)))).astype(BF16)
    branch = jnp.dot(gated, proj_ref[...], preferred_element_type=F32)
    block_ref[...] = (video_ref[...].astype(F32) + branch).astype(BF16)


def backward_kernel(place_ref, first, second, other_first, other_second, *refs):
    ext_ref, video_ref, cot_ref, temporal_ref, spread_ref = refs[:5]
    out_ref = refs[5]
    held, tail, total, sems, other_sems = refs[6:]
    core = place_ref[1]
    copies = weight_copies(place_ref, (first, second), core, held, sems, both_cores)
    copies += weight_copies(
        place_ref, (other_first, other_second), 1 - core, held, other_sems, both_cores
    )
    ext = ext_ref[...]
    nt = (((1,), (1,)), ((), ()))
    grad = lax.dot_general(ext[2 * HALO :], temporal_ref[0], nt, preferred_element_type=F32)
    grad += lax.dot_general(
        ext[HALO : HALO + ROWS], temporal_ref[1], nt, preferred_element_type=F32
    )
    grad += lax.dot_general(ext[:ROWS], temporal_ref[2], nt, preferred_element_type=F32)
    grad = grad.astype(BF16).astype(F32)
    for pair in copies:
        for copy in pair:
            copy.wait()
    last = shifted(grad, -TAPS[8][0], -TAPS[8][1]).astype(BF16)
    for tap in range(PIECES):
        moved = shifted(grad, -TAPS[tap][0], -TAPS[tap][1]).astype(BF16)
        value = lax.dot_general(moved, held[tap, :C], nt, preferred_element_type=F32)
        if tap == 0:
            total[...] = value
        else:
            total[...] += value
        tail[:, tap * TAIL : (tap + 1) * TAIL] = lax.dot_general(
            last, held[tap, C:], nt, preferred_element_type=F32
        ).astype(BF16)
    total[...] += lax.dot_general(tail[...], spread_ref[...], nt, preferred_element_type=F32)
    video = video_ref[...].astype(F32)
    out_ref[...] = (
        cot_ref[...].astype(F32) + total[...] * silu_grad(video)
    ).astype(BF16)


def whole():
    return pl.BlockSpec(memory_space=pltpu.VMEM)


def anywhere():
    return pl.BlockSpec(memory_space=pl.ANY)


def partial(place, weights, patches):
    return pl.pallas_call(
        partial_kernel,
        in_specs=[pl.BlockSpec(memory_space=pltpu.SMEM)] + [anywhere()] * 3,
        out_specs=whole(),
        out_shape=jax.ShapeDtypeStruct((EXT, C), F32),
        scratch_shapes=[
            pltpu.VMEM((4, PIECE, C), BF16),
            pltpu.VMEM((4, EXT, PIECE), BF16),
            pltpu.SemaphoreType.DMA((8,)),
            pltpu.SemaphoreType.DMA((4,)),
        ],
        compiler_params=pltpu.CompilerParams(vmem_limit_bytes=VMEM),
        cost_estimate=pl.CostEstimate(
            flops=EXT * PIECES * PIECE * C, bytes_accessed=8 * 1024 * 1024, transcendentals=0
        ),
        name="partial",
    )(place, *weights, patches)


def forward(place, weights, patches, summed, video, cot, temporal_weight, proj_weight, order):
    return pl.pallas_call(
        forward_kernel,
        in_specs=[pl.BlockSpec(memory_space=pltpu.SMEM)] + [anywhere()] * 9,
        out_specs=[whole()] * 4,
        out_shape=[
            jax.ShapeDtypeStruct((ROWS, C), BF16),
            jax.ShapeDtypeStruct((ROWS, C), BF16),
            jax.ShapeDtypeStruct((HALF, C), BF16),
            jax.ShapeDtypeStruct((HALF, C), BF16),
        ],
        scratch_shapes=[
            pltpu.VMEM((4, PIECE, C), BF16),
            pltpu.VMEM((4, EXT, PIECE), BF16),
            pltpu.VMEM((EXT, C), F32),
            pltpu.SemaphoreType.DMA((8,)),
            pltpu.SemaphoreType.DMA((4,)),
            pltpu.SemaphoreType.DMA((6,)),
            pltpu.VMEM((EXT, C), F32),
            pltpu.VMEM((ROWS, C), BF16),
            pltpu.VMEM((ROWS, C), BF16),
            pltpu.VMEM((3, C, C), BF16),
            pltpu.VMEM((C, C), BF16),
            pltpu.VMEM((C, PIECE), BF16),
        ],
        compiler_params=pltpu.CompilerParams(vmem_limit_bytes=VMEM),
        cost_estimate=pl.CostEstimate(
            flops=2 * EXT * PIECES * PIECE * C, bytes_accessed=20 * 1024 * 1024, transcendentals=0
        ),
        name="forward",
    )(place, *weights, patches, summed, video, cot, temporal_weight, proj_weight, order)


def backward(place, weights, ext, video, cot, temporal_weight, spread):
    return pl.pallas_call(
        backward_kernel,
        in_specs=[pl.BlockSpec(memory_space=pltpu.SMEM)] + [anywhere()] * 4 + [whole()] * 5,
        out_specs=whole(),
        out_shape=jax.ShapeDtypeStruct((ROWS, C), BF16),
        scratch_shapes=[
            pltpu.VMEM((PIECES, PIECE, C), BF16),
            pltpu.VMEM((ROWS, PIECES * TAIL), BF16),
            pltpu.VMEM((ROWS, C), F32),
            pltpu.SemaphoreType.DMA((8,)),
            pltpu.SemaphoreType.DMA((8,)),
        ],
        compiler_params=pltpu.CompilerParams(vmem_limit_bytes=VMEM),
        cost_estimate=pl.CostEstimate(
            flops=2 * ROWS * PIECES * PIECE * C, bytes_accessed=30 * 1024 * 1024, transcendentals=0
        ),
        name="backward",
    )(place, *weights, ext, video, cot, temporal_weight, spread)


def next_quarter(values, r):
    def step(c):
        return (0, 1, 2 if c == 0 else -2, -1)[r]

    pairs = [(c * 8 + (y + step(c)) % 8, c * 8 + y) for y in range(8) for c in range(2)]
    return lax.ppermute(values, ("c", "y"), pairs)


def over_tm(values):
    return lax.all_to_all(values, ("y", "zh"), split_axis=0, concat_axis=0, tiled=True)


def other_core(values):
    return lax.ppermute(values, "c", [(0, 1), (1, 0)])


def halos(rows):
    tm = ("y", "zh")
    before = lax.ppermute(rows[ROWS - HALO :], tm, [(t, t + 1) for t in range(TM - 1)])
    after = lax.ppermute(rows[:HALO], tm, [(t + 1, t) for t in range(TM - 1)])
    return before, after


def spread_matrix():
    k = lax.broadcasted_iota(jnp.int32, (C, PIECES * TAIL), 0)
    lane = lax.broadcasted_iota(jnp.int32, (C, PIECES * TAIL), 1)
    j, t, i = lane // TAIL, (lane % TAIL) // 8, lane % 8
    return ((i < 5) & (k == SHARD * t + 5 * j + i)).astype(BF16)


def order_matrix(core):
    k = lax.broadcasted_iota(jnp.int32, (C, PIECE), 0)
    lane = lax.broadcasted_iota(jnp.int32, (C, PIECE), 1)
    h, t, i = (lane // HALF + core) % 2, (lane % HALF) // 24, lane % 24
    return ((i < 20) & (k == SHARD * t + 20 * h + i)).astype(BF16)


def local(video, cotangent, spatial_weight, temporal_weight, proj_weight):
    core = lax.axis_index("c")
    x, y, zl = (lax.axis_index(name) for name in ("x", "y", "zl"))
    quarter = (x + y + zl) % 4
    place = jnp.stack([quarter, core, (y + zl) % 4]).astype(jnp.int32)

    rows = video.reshape(ROWS, C)
    cot = cotangent.reshape(ROWS, C)

    main = spatial_weight[:8].reshape(4, 2, SHARD, C)
    tail = spatial_weight[8].reshape(4, 2, 5, C)
    main = lax.dynamic_index_in_dim(main, core, 1, keepdims=False)
    tail = lax.dynamic_index_in_dim(tail, core, 1, keepdims=False)
    quarters = jnp.concatenate([main, tail, jnp.zeros((4, 3, C), BF16)], axis=1)
    quarters = jnp.concatenate([quarters, quarters], axis=0)
    sent = lax.dynamic_slice_in_dim(quarters, (x + zl) % 4, 4, 0)
    sent = jnp.broadcast_to(sent[None, :, None], (2, 4, 2, 48, C)).reshape(TM, 48, C)

    def rowed(got):
        width = got.shape[2]
        return jnp.concatenate(
            [got[:, :SHARD].reshape(C, width), got[:, SHARD:].reshape(TAIL, width)], axis=0
        )

    got, shared = lax.optimization_barrier((over_tm(sent), rows))
    left, right = rowed(got[:, :, :LEFT]), rowed(got[:, :, LEFT:])
    first = lax.all_to_all(
        jnp.broadcast_to(left[None], (4, PIECE, LEFT)), "x", split_axis=0, concat_axis=0, tiled=True
    )
    second = [right] + [next_quarter(right, r) for r in (1, 2, 3)]
    before, after = halos(shared)
    spread = spread_matrix()
    patches = prep(jnp.concatenate([before, rows, after], axis=0), spread)
    first, patches, *second = lax.optimization_barrier((first, patches, *second))
    weights = [first, jnp.stack(second)]
    others = [other_core(v) for v in weights]

    summed = partial(place, weights, patches)
    block_out, gated_grad, keep, give = forward(
        place, others, patches, summed, rows, cot, temporal_weight, proj_weight, order_matrix(core)
    )

    before, after = halos(gated_grad)
    pair = (keep.astype(F32) + other_core(give).astype(F32)).astype(BF16)
    blocks = over_tm(pair.reshape(TM, 24, C))
    blocks, before, after = lax.optimization_barrier((blocks, before, after))
    ext = jnp.concatenate([before, gated_grad, after], axis=0)
    video_grad = backward(place, weights + others, ext, rows, cot, temporal_weight, spread)

    block = jnp.sum(blocks.astype(F32), axis=0).astype(BF16)
    sent = jnp.broadcast_to(block[None], (16, 24, C))
    copies = lax.all_to_all(sent, ("x", "zl"), split_axis=0, concat_axis=0, tiled=True)
    copies, video_grad = lax.optimization_barrier((copies, video_grad))
    summed = jnp.sum(copies.astype(F32), axis=0)
    theirs = other_core(summed)
    low = jnp.where(core == 0, summed, theirs)[:20]
    high = jnp.where(core == 0, theirs, summed)[:20]
    factor = 1.0 / math.sqrt(ROWS * 512)
    proj_grad = jnp.concatenate([low, high], axis=0) * factor
    return (block_out.reshape(video.shape), video_grad.reshape(video.shape), proj_grad)


def solution(mesh):
    fine = Mesh(mesh.devices.reshape(4, 4, 2, 8, 2), ("x", "zl", "c", "y", "zh"))
    dp, tm = ("x", "zl", "c"), ("y", "zh")
    in_specs = (P(dp, tm, None, None), P(dp, tm, None, None), P(None, tm, None), P(), P())
    out_specs = (P(dp, tm, None, None), P(dp, tm, None, None), P(tm, None))
    return jax.shard_map(local, mesh=fine, in_specs=in_specs, out_specs=out_specs, check_vma=False)
```

```python
import functools
import math

import jax
import jax.numpy as jnp
from jax import lax
from jax.experimental import pallas as pl
from jax.experimental.pallas import tpu as pltpu
from jax.sharding import Mesh
from jax.sharding import PartitionSpec as P

C = 640
ROWS = 256
HALO = 128
EXT = ROWS + 2 * HALO
PIECE = 768
HALF = PIECE // 2
LEFT = 512
TAIL = PIECE - C
PIECES = 8
TM = 16
SHARD = 40
VMEM = 50 * 1024 * 1024
F32 = jnp.float32
BF16 = jnp.bfloat16
TAPS = [(di, dj) for di in (-1, 0, 1) for dj in (-1, 0, 1)]


def sigmoid(values):
    return 1.0 / (1.0 + jnp.exp(-values))


def silu_grad(values):
    s = sigmoid(values)
    return s * (1.0 + values * (1.0 - s))


def shifted(values, di, dj):
    rows = values.shape[0]
    step = 8 * di + dj
    moved = values if step == 0 else pltpu.roll(values, (-step) % rows, 0)
    if step == 0:
        return moved
    row = lax.broadcasted_iota(jnp.int32, values.shape, 0)
    i = (row // 8) % 8 + di
    j = row % 8 + dj
    inside = (i >= 0) & (i < 8) & (j >= 0) & (j < 8)
    return jnp.where(inside, moved, 0.0)


def prep_kernel(video_ref, spread_ref, out_ref):
    x = video_ref[...].astype(F32)
    act = (x * sigmoid(x)).astype(BF16).astype(F32)
    last = shifted(act, *TAPS[8]).astype(BF16)
    tail = jnp.dot(last, spread_ref[...], preferred_element_type=F32).astype(BF16)
    for tap in range(PIECES):
        out_ref[tap, :, :C] = shifted(act, *TAPS[tap]).astype(BF16)
        out_ref[tap, :, C:] = tail[:, tap * TAIL : (tap + 1) * TAIL]


def prep(video_ext, spread):
    chunk = 128
    return pl.pallas_call(
        prep_kernel,
        grid=(EXT // chunk,),
        in_specs=[
            pl.BlockSpec((chunk, C), lambda n: (n, 0)),
            pl.BlockSpec((C, PIECES * TAIL), lambda n: (0, 0)),
        ],
        out_specs=pl.BlockSpec((PIECES, chunk, PIECE), lambda n: (0, n, 0)),
        out_shape=jax.ShapeDtypeStruct((PIECES, EXT, PIECE), BF16),
        compiler_params=pltpu.CompilerParams(vmem_limit_bytes=VMEM),
        cost_estimate=pl.CostEstimate(flops=16 * EXT * C * PIECES * TAIL, bytes_accessed=20 * 1024 * 1024, transcendentals=0),
        name="patches",
    )(video_ext, spread)


def weight_copies(
    place_ref, refs, which, held, sems, index, patch_ref=None, patches=None, patch_sems=None
):
    own, start = place_ref[0], place_ref[2]
    first, second = refs
    copies = []
    for quarter in range(4):
        from_x = (quarter - start + 4) % 4
        from_y = (quarter - own + 4) % 4
        slot = index(quarter, which)
        pair = [
            pltpu.make_async_copy(
                first.at[from_x], held.at[slot, :, pl.ds(0, LEFT)], sems.at[2 * quarter]
            ),
            pltpu.make_async_copy(
                second.at[from_y], held.at[slot, :, pl.ds(LEFT, C - LEFT)], sems.at[2 * quarter + 1]
            ),
        ]
        if patch_ref is not None:
            pair.append(
                pltpu.make_async_copy(
                    patch_ref.at[2 * quarter + which], patches.at[quarter], patch_sems.at[quarter]
                )
            )
        for copy in pair:
            copy.start()
        copies.append(pair)
    return copies


def spatial_sum(patches, held, copies, total):
    for quarter in range(4):
        for copy in copies[quarter]:
            copy.wait()
        value = jnp.dot(patches[quarter], held[quarter], preferred_element_type=F32)
        if quarter == 0:
            total[...] = value
        else:
            total[...] += value


def one_core(quarter, which):
    return quarter


def both_cores(quarter, which):
    return 2 * quarter + which


def partial_kernel(place_ref, first, second, patch_ref, out_ref, held, patches, sems, patch_sems):
    core = place_ref[1]
    copies = weight_copies(
        place_ref, (first, second), core, held, sems, one_core, patch_ref, patches, patch_sems
    )
    spatial_sum(patches, held, copies, out_ref)


def forward_kernel(place_ref, first, second, patch_ref, *refs):
    given = refs[:6]
    block_ref, gg_ref, keep_ref, give_ref = refs[6:10]
    held, patches, total, sems, patch_sems, given_sems = refs[10:16]
    local = refs[16:]
    partial_ref, video_ref, cot_ref, temporal_ref, proj_ref, order_ref = local
    core = 1 - place_ref[1]
    copies = weight_copies(
        place_ref, (first, second), core, held, sems, one_core, patch_ref, patches, patch_sems
    )
    later = [
        pltpu.make_async_copy(given[n], local[n], given_sems.at[n]) for n in range(len(given))
    ]
    for copy in later:
        copy.start()
    spatial_sum(patches, held, copies, total)
    for copy in later:
        copy.wait()
    total = total[...] + partial_ref[...]
    spatial = total.astype(BF16)
    temporal = jnp.dot(spatial[:ROWS], temporal_ref[0], preferred_element_type=F32)
    for m in (1, 2):
        temporal += jnp.dot(
            spatial[m * HALO : m * HALO + ROWS], temporal_ref[m], preferred_element_type=F32
        )
    temporal = temporal.astype(BF16).astype(F32)
    s = sigmoid(temporal)
    gated = (temporal * s).astype(BF16)
    cot = cot_ref[...]
    ordered = jnp.dot(gated, order_ref[...], preferred_element_type=F32).astype(BF16)
    part = lax.dot_general(
        ordered, cot, (((0,), (0,)), ((), ())), preferred_element_type=F32
    ).astype(BF16)
    keep_ref[...] = part[:HALF]
    give_ref[...] = part[HALF:]
    back = lax.dot_general(
        cot, proj_ref[...], (((1,), (1,)), ((), ())), preferred_element_type=F32
    )
    gg_ref[...] = (back * (s * (1.0 + temporal * (1.0 - s)))).astype(BF16)
    branch = jnp.dot(gated, proj_ref[...], preferred_element_type=F32)
    block_ref[...] = (video_ref[...].astype(F32) + branch).astype(BF16)


def backward_kernel(place_ref, first, second, other_first, other_second, *refs):
    ext_ref, video_ref, cot_ref, temporal_ref, spread_ref = refs[:5]
    out_ref = refs[5]
    held, tail, total, sems, other_sems = refs[6:]
    core = place_ref[1]
    copies = weight_copies(place_ref, (first, second), core, held, sems, both_cores)
    copies += weight_copies(
        place_ref, (other_first, other_second), 1 - core, held, other_sems, both_cores
    )
    ext = ext_ref[...]
    nt = (((1,), (1,)), ((), ()))
    grad = lax.dot_general(ext[2 * HALO :], temporal_ref[0], nt, preferred_element_type=F32)
    grad += lax.dot_general(
        ext[HALO : HALO + ROWS], temporal_ref[1], nt, preferred_element_type=F32
    )
    grad += lax.dot_general(ext[:ROWS], temporal_ref[2], nt, preferred_element_type=F32)
    grad = grad.astype(BF16).astype(F32)
    for pair in copies:
        for copy in pair:
            copy.wait()
    last = shifted(grad, -TAPS[8][0], -TAPS[8][1]).astype(BF16)
    for tap in range(PIECES):
        moved = shifted(grad, -TAPS[tap][0], -TAPS[tap][1]).astype(BF16)
        value = lax.dot_general(moved, held[tap, :C], nt, preferred_element_type=F32)
        if tap == 0:
            total[...] = value
        else:
            total[...] += value
        tail[:, tap * TAIL : (tap + 1) * TAIL] = lax.dot_general(
            last, held[tap, C:], nt, preferred_element_type=F32
        ).astype(BF16)
    total[...] += lax.dot_general(tail[...], spread_ref[...], nt, preferred_element_type=F32)
    video = video_ref[...].astype(F32)
    out_ref[...] = (
        cot_ref[...].astype(F32) + total[...] * silu_grad(video)
    ).astype(BF16)


def whole():
    return pl.BlockSpec(memory_space=pltpu.VMEM)


def anywhere():
    return pl.BlockSpec(memory_space=pl.ANY)


def partial(place, weights, patches):
    return pl.pallas_call(
        partial_kernel,
        in_specs=[pl.BlockSpec(memory_space=pltpu.SMEM)] + [anywhere()] * 3,
        out_specs=whole(),
        out_shape=jax.ShapeDtypeStruct((EXT, C), F32),
        scratch_shapes=[
            pltpu.VMEM((4, PIECE, C), BF16),
            pltpu.VMEM((4, EXT, PIECE), BF16),
            pltpu.SemaphoreType.DMA((8,)),
            pltpu.SemaphoreType.DMA((4,)),
        ],
        compiler_params=pltpu.CompilerParams(vmem_limit_bytes=VMEM),
        cost_estimate=pl.CostEstimate(
            flops=EXT * PIECES * PIECE * C, bytes_accessed=8 * 1024 * 1024, transcendentals=0
        ),
        name="partial",
    )(place, *weights, patches)


def forward(place, weights, patches, summed, video, cot, temporal_weight, proj_weight, order):
    return pl.pallas_call(
        forward_kernel,
        in_specs=[pl.BlockSpec(memory_space=pltpu.SMEM)] + [anywhere()] * 9,
        out_specs=[whole()] * 4,
        out_shape=[
            jax.ShapeDtypeStruct((ROWS, C), BF16),
            jax.ShapeDtypeStruct((ROWS, C), BF16),
            jax.ShapeDtypeStruct((HALF, C), BF16),
            jax.ShapeDtypeStruct((HALF, C), BF16),
        ],
        scratch_shapes=[
            pltpu.VMEM((4, PIECE, C), BF16),
            pltpu.VMEM((4, EXT, PIECE), BF16),
            pltpu.VMEM((EXT, C), F32),
            pltpu.SemaphoreType.DMA((8,)),
            pltpu.SemaphoreType.DMA((4,)),
            pltpu.SemaphoreType.DMA((6,)),
            pltpu.VMEM((EXT, C), F32),
            pltpu.VMEM((ROWS, C), BF16),
            pltpu.VMEM((ROWS, C), BF16),
            pltpu.VMEM((3, C, C), BF16),
            pltpu.VMEM((C, C), BF16),
            pltpu.VMEM((C, PIECE), BF16),
        ],
        compiler_params=pltpu.CompilerParams(vmem_limit_bytes=VMEM),
        cost_estimate=pl.CostEstimate(
            flops=2 * EXT * PIECES * PIECE * C, bytes_accessed=20 * 1024 * 1024, transcendentals=0
        ),
        name="forward",
    )(place, *weights, patches, summed, video, cot, temporal_weight, proj_weight, order)


def backward(place, weights, ext, video, cot, temporal_weight, spread):
    return pl.pallas_call(
        backward_kernel,
        in_specs=[pl.BlockSpec(memory_space=pltpu.SMEM)] + [anywhere()] * 4 + [whole()] * 5,
        out_specs=whole(),
        out_shape=jax.ShapeDtypeStruct((ROWS, C), BF16),
        scratch_shapes=[
            pltpu.VMEM((PIECES, PIECE, C), BF16),
            pltpu.VMEM((ROWS, PIECES * TAIL), BF16),
            pltpu.VMEM((ROWS, C), F32),
            pltpu.SemaphoreType.DMA((8,)),
            pltpu.SemaphoreType.DMA((8,)),
        ],
        compiler_params=pltpu.CompilerParams(vmem_limit_bytes=VMEM),
        cost_estimate=pl.CostEstimate(
            flops=2 * ROWS * PIECES * PIECE * C, bytes_accessed=30 * 1024 * 1024, transcendentals=0
        ),
        name="backward",
    )(place, *weights, ext, video, cot, temporal_weight, spread)


def next_quarter(values, r):
    def step(c):
        return (0, 1, 2 if c == 0 else -2, -1)[r]

    pairs = [(c * 8 + (y + step(c)) % 8, c * 8 + y) for y in range(8) for c in range(2)]
    return lax.ppermute(values, ("c", "y"), pairs)


def over_tm(values):
    return lax.all_to_all(values, ("y", "zh"), split_axis=0, concat_axis=0, tiled=True)


def paired(values):
    groups = [
        [(zl if zh == 0 else 3 - zl) * 16 + y * 2 + zh for y in range(8) for zh in range(2)]
        for zl in range(4)
    ]
    return lax.all_to_all(
        values, ("zl", "y", "zh"), split_axis=0, concat_axis=0, axis_index_groups=groups, tiled=True
    )


def other_core(values):
    return lax.ppermute(values, "c", [(0, 1), (1, 0)])


def halos(rows):
    tm = ("y", "zh")
    before = lax.ppermute(rows[ROWS - HALO :], tm, [(t, t + 1) for t in range(TM - 1)])
    after = lax.ppermute(rows[:HALO], tm, [(t + 1, t) for t in range(TM - 1)])
    return before, after


def spread_matrix():
    k = lax.broadcasted_iota(jnp.int32, (C, PIECES * TAIL), 0)
    lane = lax.broadcasted_iota(jnp.int32, (C, PIECES * TAIL), 1)
    j, t, i = lane // TAIL, (lane % TAIL) // 8, lane % 8
    return ((i < 5) & (k == SHARD * t + 5 * j + i)).astype(BF16)


def order_matrix(core):
    k = lax.broadcasted_iota(jnp.int32, (C, PIECE), 0)
    lane = lax.broadcasted_iota(jnp.int32, (C, PIECE), 1)
    h, t, i = (lane // HALF + core) % 2, (lane % HALF) // 24, lane % 24
    return ((i < 20) & (k == SHARD * t + 20 * h + i)).astype(BF16)


def local(video, cotangent, spatial_weight, temporal_weight, proj_weight):
    core = lax.axis_index("c")
    x, y, zl, zh = (lax.axis_index(name) for name in ("x", "y", "zl", "zh"))
    quarter = (x + y + zl) % 4
    place = jnp.stack([quarter, core, (y + zl) % 4]).astype(jnp.int32)

    rows = video.reshape(ROWS, C)
    cot = cotangent.reshape(ROWS, C)

    main = spatial_weight[:8].reshape(4, 2, SHARD, C)
    tail = spatial_weight[8].reshape(4, 2, 5, C)
    main = lax.dynamic_index_in_dim(main, core, 1, keepdims=False)
    tail = lax.dynamic_index_in_dim(tail, core, 1, keepdims=False)
    quarters = jnp.concatenate([main, tail, jnp.zeros((4, 3, C), BF16)], axis=1)
    quarters = jnp.concatenate([quarters, quarters], axis=0)
    low = lax.dynamic_slice_in_dim(quarters, (x + jnp.where(zh == 0, zl, 3 - zl)) % 4, 4, 0)
    high = lax.dynamic_slice_in_dim(quarters, (x + jnp.where(zh == 0, 3 - zl, zl)) % 4, 4, 0)
    sent = jnp.stack([low, high], axis=1)
    sent = jnp.broadcast_to(sent[None], (2, 4, 2, 48, C)).reshape(TM, 48, C)

    def rowed(got):
        width = got.shape[2]
        return jnp.concatenate(
            [got[:, :SHARD].reshape(C, width), got[:, SHARD:].reshape(TAIL, width)], axis=0
        )

    got, shared = lax.optimization_barrier((paired(sent), rows))
    left, right = rowed(got[:, :, :LEFT]), rowed(got[:, :, LEFT:])
    first = lax.all_to_all(
        jnp.broadcast_to(left[None], (4, PIECE, LEFT)), "x", split_axis=0, concat_axis=0, tiled=True
    )
    second = [right] + [next_quarter(right, r) for r in (1, 2, 3)]
    before, after = halos(shared)
    spread = spread_matrix()
    patches = prep(jnp.concatenate([before, rows, after], axis=0), spread)
    patches, *second = lax.optimization_barrier((patches, *second))
    second = jnp.stack(second)
    first, other_second = lax.optimization_barrier((first, other_core(second)))
    weights = [first, second]
    others = [other_core(first), other_second]

    summed = partial(place, weights, patches)
    block_out, gated_grad, keep, give = forward(
        place, others, patches, summed, rows, cot, temporal_weight, proj_weight, order_matrix(core)
    )

    before, after = halos(gated_grad)
    pair = (keep.astype(F32) + other_core(give).astype(F32)).astype(BF16)
    blocks = over_tm(pair.reshape(TM, 24, C))
    blocks, before, after = lax.optimization_barrier((blocks, before, after))
    ext = jnp.concatenate([before, gated_grad, after], axis=0)
    video_grad = backward(place, weights + others, ext, rows, cot, temporal_weight, spread)

    block = jnp.sum(blocks.astype(F32), axis=0).astype(BF16)
    sent = jnp.broadcast_to(block[None], (16, 24, C))
    copies = lax.all_to_all(sent, ("x", "zl"), split_axis=0, concat_axis=0, tiled=True)
    copies, video_grad = lax.optimization_barrier((copies, video_grad))
    summed = jnp.sum(copies.astype(F32), axis=0)
    theirs = other_core(summed)
    low = jnp.where(core == 0, summed, theirs)[:20]
    high = jnp.where(core == 0, theirs, summed)[:20]
    factor = 1.0 / math.sqrt(ROWS * 512)
    proj_grad = jnp.concatenate([low, high], axis=0) * factor
    return (block_out.reshape(video.shape), video_grad.reshape(video.shape), proj_grad)


def solution(mesh):
    fine = Mesh(mesh.devices.reshape(4, 4, 2, 8, 2), ("x", "zl", "c", "y", "zh"))
    dp, tm = ("x", "zl", "c"), ("y", "zh")
    in_specs = (P(dp, tm, None, None), P(dp, tm, None, None), P(None, tm, None), P(), P())
    out_specs = (P(dp, tm, None, None), P(dp, tm, None, None), P(tm, None))
    return jax.shard_map(local, mesh=fine, in_specs=in_specs, out_specs=out_specs, check_vma=False)
```

```python
import functools
import math

import jax
import jax.numpy as jnp
from jax import lax
from jax.experimental import pallas as pl
from jax.experimental.pallas import tpu as pltpu
from jax.sharding import Mesh
from jax.sharding import PartitionSpec as P

C = 640
ROWS = 256
HALO = 128
EXT = ROWS + 2 * HALO
PIECE = 768
HALF = PIECE // 2
LEFT = 512
TAIL = PIECE - C
PIECES = 8
TM = 16
SHARD = 40
VMEM = 50 * 1024 * 1024
F32 = jnp.float32
BF16 = jnp.bfloat16
TAPS = [(di, dj) for di in (-1, 0, 1) for dj in (-1, 0, 1)]


def sigmoid(values):
    return 1.0 / (1.0 + jnp.exp(-values))


def silu_grad(values):
    s = sigmoid(values)
    return s * (1.0 + values * (1.0 - s))


def shifted(values, di, dj):
    rows = values.shape[0]
    step = 8 * di + dj
    moved = values if step == 0 else pltpu.roll(values, (-step) % rows, 0)
    if step == 0:
        return moved
    row = lax.broadcasted_iota(jnp.int32, values.shape, 0)
    i = (row // 8) % 8 + di
    j = row % 8 + dj
    inside = (i >= 0) & (i < 8) & (j >= 0) & (j < 8)
    return jnp.where(inside, moved, 0.0)


def prep_kernel(video_ref, spread_ref, out_ref):
    x = video_ref[...].astype(F32)
    act = (x * sigmoid(x)).astype(BF16).astype(F32)
    last = shifted(act, *TAPS[8]).astype(BF16)
    tail = jnp.dot(last, spread_ref[...], preferred_element_type=F32).astype(BF16)
    for tap in range(PIECES):
        out_ref[tap, :, :C] = shifted(act, *TAPS[tap]).astype(BF16)
        out_ref[tap, :, C:] = tail[:, tap * TAIL : (tap + 1) * TAIL]


def prep(video_ext, spread):
    chunk = 128
    return pl.pallas_call(
        prep_kernel,
        grid=(EXT // chunk,),
        in_specs=[
            pl.BlockSpec((chunk, C), lambda n: (n, 0)),
            pl.BlockSpec((C, PIECES * TAIL), lambda n: (0, 0)),
        ],
        out_specs=pl.BlockSpec((PIECES, chunk, PIECE), lambda n: (0, n, 0)),
        out_shape=jax.ShapeDtypeStruct((PIECES, EXT, PIECE), BF16),
        compiler_params=pltpu.CompilerParams(vmem_limit_bytes=VMEM),
        cost_estimate=pl.CostEstimate(flops=16 * EXT * C * PIECES * TAIL, bytes_accessed=20 * 1024 * 1024, transcendentals=0),
        name="patches",
    )(video_ext, spread)


def weight_copies(
    place_ref, refs, which, held, sems, index, patch_ref=None, patches=None, patch_sems=None
):
    own, start = place_ref[0], place_ref[2]
    first, second = refs
    copies = []
    for quarter in range(4):
        from_x = (quarter - start + 4) % 4
        from_y = (quarter - own + 4) % 4
        slot = index(quarter, which)
        pair = [
            pltpu.make_async_copy(
                first.at[from_x], held.at[slot, :, pl.ds(0, LEFT)], sems.at[2 * quarter]
            ),
            pltpu.make_async_copy(
                second.at[from_y], held.at[slot, :, pl.ds(LEFT, C - LEFT)], sems.at[2 * quarter + 1]
            ),
        ]
        if patch_ref is not None:
            pair.append(
                pltpu.make_async_copy(
                    patch_ref.at[2 * quarter + which], patches.at[quarter], patch_sems.at[quarter]
                )
            )
        for copy in pair:
            copy.start()
        copies.append(pair)
    return copies


def spatial_sum(patches, held, copies, total):
    for quarter in range(4):
        for copy in copies[quarter]:
            copy.wait()
        value = jnp.dot(patches[quarter], held[quarter], preferred_element_type=F32)
        if quarter == 0:
            total[...] = value
        else:
            total[...] += value


def one_core(quarter, which):
    return quarter


def both_cores(quarter, which):
    return 2 * quarter + which


def partial_kernel(place_ref, first, second, patch_ref, out_ref, held, patches, sems, patch_sems):
    core = place_ref[1]
    copies = weight_copies(
        place_ref, (first, second), core, held, sems, one_core, patch_ref, patches, patch_sems
    )
    spatial_sum(patches, held, copies, out_ref)


def forward_kernel(place_ref, first, second, patch_ref, *refs):
    given = refs[:6]
    block_ref, gg_ref, keep_ref, give_ref = refs[6:10]
    held, patches, total, sems, patch_sems, given_sems = refs[10:16]
    local = refs[16:]
    partial_ref, video_ref, cot_ref, temporal_ref, proj_ref, order_ref = local
    core = 1 - place_ref[1]
    copies = weight_copies(
        place_ref, (first, second), core, held, sems, one_core, patch_ref, patches, patch_sems
    )
    later = [
        pltpu.make_async_copy(given[n], local[n], given_sems.at[n]) for n in range(len(given))
    ]
    for copy in later:
        copy.start()
    spatial_sum(patches, held, copies, total)
    for copy in later:
        copy.wait()
    total = total[...] + partial_ref[...]
    spatial = total.astype(BF16)
    temporal = jnp.dot(spatial[:ROWS], temporal_ref[0], preferred_element_type=F32)
    for m in (1, 2):
        temporal += jnp.dot(
            spatial[m * HALO : m * HALO + ROWS], temporal_ref[m], preferred_element_type=F32
        )
    temporal = temporal.astype(BF16).astype(F32)
    s = sigmoid(temporal)
    gated = (temporal * s).astype(BF16)
    cot = cot_ref[...]
    ordered = jnp.dot(gated, order_ref[...], preferred_element_type=F32).astype(BF16)
    part = lax.dot_general(
        ordered, cot, (((0,), (0,)), ((), ())), preferred_element_type=F32
    ).astype(BF16)
    keep_ref[...] = part[:HALF]
    give_ref[...] = part[HALF:]
    back = lax.dot_general(
        cot, proj_ref[...], (((1,), (1,)), ((), ())), preferred_element_type=F32
    )
    gg_ref[...] = (back * (s * (1.0 + temporal * (1.0 - s)))).astype(BF16)
    branch = jnp.dot(gated, proj_ref[...], preferred_element_type=F32)
    block_ref[...] = (video_ref[...].astype(F32) + branch).astype(BF16)


def backward_kernel(place_ref, first, second, other_first, other_second, *refs):
    ext_ref, video_ref, cot_ref, temporal_ref, spread_ref = refs[:5]
    out_ref = refs[5]
    held, tail, total, sems, other_sems = refs[6:]
    core = place_ref[1]
    copies = weight_copies(place_ref, (first, second), core, held, sems, both_cores)
    copies += weight_copies(
        place_ref, (other_first, other_second), 1 - core, held, other_sems, both_cores
    )
    ext = ext_ref[...]
    nt = (((1,), (1,)), ((), ()))
    grad = lax.dot_general(ext[2 * HALO :], temporal_ref[0], nt, preferred_element_type=F32)
    grad += lax.dot_general(
        ext[HALO : HALO + ROWS], temporal_ref[1], nt, preferred_element_type=F32
    )
    grad += lax.dot_general(ext[:ROWS], temporal_ref[2], nt, preferred_element_type=F32)
    grad = grad.astype(BF16).astype(F32)
    for pair in copies:
        for copy in pair:
            copy.wait()
    last = shifted(grad, -TAPS[8][0], -TAPS[8][1]).astype(BF16)
    for tap in range(PIECES):
        moved = shifted(grad, -TAPS[tap][0], -TAPS[tap][1]).astype(BF16)
        value = lax.dot_general(moved, held[tap, :C], nt, preferred_element_type=F32)
        if tap == 0:
            total[...] = value
        else:
            total[...] += value
        tail[:, tap * TAIL : (tap + 1) * TAIL] = lax.dot_general(
            last, held[tap, C:], nt, preferred_element_type=F32
        ).astype(BF16)
    total[...] += lax.dot_general(tail[...], spread_ref[...], nt, preferred_element_type=F32)
    video = video_ref[...].astype(F32)
    out_ref[...] = (
        cot_ref[...].astype(F32) + total[...] * silu_grad(video)
    ).astype(BF16)


def whole():
    return pl.BlockSpec(memory_space=pltpu.VMEM)


def anywhere():
    return pl.BlockSpec(memory_space=pl.ANY)


def partial(place, weights, patches):
    return pl.pallas_call(
        partial_kernel,
        in_specs=[pl.BlockSpec(memory_space=pltpu.SMEM)] + [anywhere()] * 3,
        out_specs=whole(),
        out_shape=jax.ShapeDtypeStruct((EXT, C), F32),
        scratch_shapes=[
            pltpu.VMEM((4, PIECE, C), BF16),
            pltpu.VMEM((4, EXT, PIECE), BF16),
            pltpu.SemaphoreType.DMA((8,)),
            pltpu.SemaphoreType.DMA((4,)),
        ],
        compiler_params=pltpu.CompilerParams(vmem_limit_bytes=VMEM),
        cost_estimate=pl.CostEstimate(
            flops=EXT * PIECES * PIECE * C, bytes_accessed=8 * 1024 * 1024, transcendentals=0
        ),
        name="partial",
    )(place, *weights, patches)


def forward(place, weights, patches, summed, video, cot, temporal_weight, proj_weight, order):
    return pl.pallas_call(
        forward_kernel,
        in_specs=[pl.BlockSpec(memory_space=pltpu.SMEM)] + [anywhere()] * 9,
        out_specs=[whole()] * 4,
        out_shape=[
            jax.ShapeDtypeStruct((ROWS, C), BF16),
            jax.ShapeDtypeStruct((ROWS, C), BF16),
            jax.ShapeDtypeStruct((HALF, C), BF16),
            jax.ShapeDtypeStruct((HALF, C), BF16),
        ],
        scratch_shapes=[
            pltpu.VMEM((4, PIECE, C), BF16),
            pltpu.VMEM((4, EXT, PIECE), BF16),
            pltpu.VMEM((EXT, C), F32),
            pltpu.SemaphoreType.DMA((8,)),
            pltpu.SemaphoreType.DMA((4,)),
            pltpu.SemaphoreType.DMA((6,)),
            pltpu.VMEM((EXT, C), F32),
            pltpu.VMEM((ROWS, C), BF16),
            pltpu.VMEM((ROWS, C), BF16),
            pltpu.VMEM((3, C, C), BF16),
            pltpu.VMEM((C, C), BF16),
            pltpu.VMEM((C, PIECE), BF16),
        ],
        compiler_params=pltpu.CompilerParams(vmem_limit_bytes=VMEM),
        cost_estimate=pl.CostEstimate(
            flops=2 * EXT * PIECES * PIECE * C, bytes_accessed=20 * 1024 * 1024, transcendentals=0
        ),
        name="forward",
    )(place, *weights, patches, summed, video, cot, temporal_weight, proj_weight, order)


def backward(place, weights, ext, video, cot, temporal_weight, spread):
    return pl.pallas_call(
        backward_kernel,
        in_specs=[pl.BlockSpec(memory_space=pltpu.SMEM)] + [anywhere()] * 4 + [whole()] * 5,
        out_specs=whole(),
        out_shape=jax.ShapeDtypeStruct((ROWS, C), BF16),
        scratch_shapes=[
            pltpu.VMEM((PIECES, PIECE, C), BF16),
            pltpu.VMEM((ROWS, PIECES * TAIL), BF16),
            pltpu.VMEM((ROWS, C), F32),
            pltpu.SemaphoreType.DMA((8,)),
            pltpu.SemaphoreType.DMA((8,)),
        ],
        compiler_params=pltpu.CompilerParams(vmem_limit_bytes=VMEM),
        cost_estimate=pl.CostEstimate(
            flops=2 * ROWS * PIECES * PIECE * C, bytes_accessed=30 * 1024 * 1024, transcendentals=0
        ),
        name="backward",
    )(place, *weights, ext, video, cot, temporal_weight, spread)


def next_quarter(values, r):
    def step(c):
        return (0, 1, 2 if c == 0 else -2, -1)[r]

    pairs = [(c * 8 + (y + step(c)) % 8, c * 8 + y) for y in range(8) for c in range(2)]
    return lax.ppermute(values, ("c", "y"), pairs)


def paired(values):
    groups = [
        [(zl if zh == 0 else 3 - zl) * 16 + y * 2 + zh for y in range(8) for zh in range(2)]
        for zl in range(4)
    ]
    return lax.all_to_all(
        values, ("zl", "y", "zh"), split_axis=0, concat_axis=0, axis_index_groups=groups, tiled=True
    )


def other_core(values):
    return lax.ppermute(values, "c", [(0, 1), (1, 0)])


def halos(rows):
    tm = ("y", "zh")
    before = lax.ppermute(rows[ROWS - HALO :], tm, [(t, t + 1) for t in range(TM - 1)])
    after = lax.ppermute(rows[:HALO], tm, [(t + 1, t) for t in range(TM - 1)])
    return before, after


def spread_matrix():
    k = lax.broadcasted_iota(jnp.int32, (C, PIECES * TAIL), 0)
    lane = lax.broadcasted_iota(jnp.int32, (C, PIECES * TAIL), 1)
    j, t, i = lane // TAIL, (lane % TAIL) // 8, lane % 8
    return ((i < 5) & (k == SHARD * t + 5 * j + i)).astype(BF16)


def order_matrix(core):
    k = lax.broadcasted_iota(jnp.int32, (C, PIECE), 0)
    lane = lax.broadcasted_iota(jnp.int32, (C, PIECE), 1)
    h, t, i = (lane // HALF + core) % 2, (lane % HALF) // 24, lane % 24
    return ((i < 20) & (k == SHARD * t + 20 * h + i)).astype(BF16)


def local(video, cotangent, spatial_weight, temporal_weight, proj_weight):
    core = lax.axis_index("c")
    x, y, zl, zh = (lax.axis_index(name) for name in ("x", "y", "zl", "zh"))
    quarter = (x + y + zl) % 4
    place = jnp.stack([quarter, core, (y + zl) % 4]).astype(jnp.int32)

    rows = video.reshape(ROWS, C)
    cot = cotangent.reshape(ROWS, C)

    main = spatial_weight[:8].reshape(4, 2, SHARD, C)
    tail = spatial_weight[8].reshape(4, 2, 5, C)
    main = lax.dynamic_index_in_dim(main, core, 1, keepdims=False)
    tail = lax.dynamic_index_in_dim(tail, core, 1, keepdims=False)
    quarters = jnp.concatenate([main, tail, jnp.zeros((4, 3, C), BF16)], axis=1)
    quarters = jnp.concatenate([quarters, quarters], axis=0)
    low = lax.dynamic_slice_in_dim(quarters, (x + jnp.where(zh == 0, zl, 3 - zl)) % 4, 4, 0)
    high = lax.dynamic_slice_in_dim(quarters, (x + jnp.where(zh == 0, 3 - zl, zl)) % 4, 4, 0)
    sent = jnp.stack([low, high], axis=1)
    sent = jnp.broadcast_to(sent[None], (2, 4, 2, 48, C)).reshape(TM, 48, C)

    def rowed(got):
        width = got.shape[2]
        return jnp.concatenate(
            [got[:, :SHARD].reshape(C, width), got[:, SHARD:].reshape(TAIL, width)], axis=0
        )

    got, shared = lax.optimization_barrier((paired(sent), rows))
    left, right = rowed(got[:, :, :LEFT]), rowed(got[:, :, LEFT:])
    first = lax.all_to_all(
        jnp.broadcast_to(left[None], (4, PIECE, LEFT)), "x", split_axis=0, concat_axis=0, tiled=True
    )
    second = [right] + [next_quarter(right, r) for r in (1, 2, 3)]
    before, after = halos(shared)
    spread = spread_matrix()
    patches = prep(jnp.concatenate([before, rows, after], axis=0), spread)
    patches, *second = lax.optimization_barrier((patches, *second))
    second = jnp.stack(second)
    first, other_second = lax.optimization_barrier((first, other_core(second)))
    weights = [first, second]
    others = [other_core(first), other_second]

    summed = partial(place, weights, patches)
    block_out, gated_grad, keep, give = forward(
        place, others, patches, summed, rows, cot, temporal_weight, proj_weight, order_matrix(core)
    )

    before, after = halos(gated_grad)
    pair = (keep.astype(F32) + other_core(give).astype(F32)).astype(BF16)
    blocks = paired(pair.reshape(TM, 24, C))
    blocks, before, after = lax.optimization_barrier((blocks, before, after))
    ext = jnp.concatenate([before, gated_grad, after], axis=0)
    video_grad = backward(place, weights + others, ext, rows, cot, temporal_weight, spread)

    block = jnp.sum(blocks.astype(F32), axis=0).astype(BF16)
    sent = jnp.broadcast_to(block[None], (16, 24, C))
    copies = lax.all_to_all(sent, ("x", "zl"), split_axis=0, concat_axis=0, tiled=True)
    copies, video_grad = lax.optimization_barrier((copies, video_grad))
    summed = jnp.sum(copies.astype(F32), axis=0)
    theirs = other_core(summed)
    low = jnp.where(core == 0, summed, theirs)[:20]
    high = jnp.where(core == 0, theirs, summed)[:20]
    factor = 1.0 / math.sqrt(ROWS * 512)
    proj_grad = jnp.concatenate([low, high], axis=0) * factor
    return (block_out.reshape(video.shape), video_grad.reshape(video.shape), proj_grad)


def solution(mesh):
    fine = Mesh(mesh.devices.reshape(4, 4, 2, 8, 2), ("x", "zl", "c", "y", "zh"))
    dp, tm = ("x", "zl", "c"), ("y", "zh")
    in_specs = (P(dp, tm, None, None), P(dp, tm, None, None), P(None, tm, None), P(), P())
    out_specs = (P(dp, tm, None, None), P(dp, tm, None, None), P(tm, None))
    return jax.shard_map(local, mesh=fine, in_specs=in_specs, out_specs=out_specs, check_vma=False)
```
